128 devices in a mesh: seq: 64 (over z_lo, x, y, core), tp: 2 (over z_hi).
Axes of the slice: x: 4, y: 4, z: 4 (z_hi: 2, z_lo: 2; z = z_hi * 2 + z_lo), core: 2. Of those that a mesh axis runs over, the one named last changes fastest.
Arguments:
- hidden: bfloat16 [65536, 1408], P('seq'), may hold values from -8.5 to 8.5
- out_cotangent: bfloat16 [65536, 1408], P('seq'), may hold values from -6 to 6
- qkv_weight: bfloat16 [1408, 3, 1408], P(None, None, 'tp'), may hold values from -0.15625 to 0.15625
- out_weight: bfloat16 [1408, 1408], P('tp'), may hold values from -0.15625 to 0.15625
Outputs:
- grad_hidden: bfloat16 [65536, 1408], P('seq', 'tp')
- qkv_grad: float32 [1408, 3, 1408], P('seq', None, 'tp')
- out_grad: float32 [1408, 1408], P(('tp', 'seq'))
The draws below stay inside these ranges and needn't reach their ends.
All inputs are finite; a program needn't handle non-finite values.
Results may differ from the reference program's by a relative error of at most 0.015.
The reference program's roundings to bfloat16 on the way (of `qkv`, `grad_attn`, `weights`, `attn`, `dscores` and `dqkv`) count: a program that leaves them out, or rounds other values in their place, can miss the bound.
Values may be sent and summed in bfloat16 or wider, within the bound.
No kernel may reach another device: no remote copies, remote signals or barrier semaphores. Data moves between devices by JAX's collectives and lax.ppermute only.
A program may use at most 192 MiB of HBM per device.

```python
import jax
import jax.numpy as jnp
from jax import lax

HEADS = 16
HEAD_DIM = 88
P_SIZE = 256
D = 1408
FRAMES = 256
TOKENS = 65536


def draw_hidden(key, part):
    key = jax.random.fold_in(key, 11)
    values = jax.random.normal(key, (TOKENS, D), jnp.float32)
    return jnp.clip(values, -6.0, 6.0).astype(jnp.bfloat16)


def block_scale(key, extent, cuts, least, top_value):
    level, own = 1.0, jax.random.fold_in(key, 6)
    for axis_at, blocks in cuts:
        steps = jnp.exp(jax.random.uniform(jax.random.fold_in(own, axis_at), (blocks,), jnp.float32, least / len(cuts), top_value / len(cuts)))
        level = level * jnp.repeat(steps, extent[axis_at] // blocks).reshape([-1 if axis == axis_at else 1 for axis in range(len(extent))])
    return level


def centred(stream_key, extent, width, bound, cuts=(), held_as=jnp.bfloat16):
    loudness = block_scale(stream_key, extent, cuts, -0.22, 0.18) if cuts else 1.0
    result = jax.random.normal(stream_key, extent, jnp.float32) * width * loudness
    return jnp.minimum(jnp.maximum(result, -bound), bound).astype(held_as)


def setup_inputs(seed: int = 0) -> dict:
    key_of = jax.random.split(jax.random.key(seed), 5)
    return {
        "hidden": draw_hidden(jax.random.fold_in(key_of[4], 71), 0),
        "out_cotangent": centred(key_of[1], (TOKENS, D), 1.0, 6.0, ((0, 64),)),
        "qkv_weight": centred(key_of[2], (D, 3, D), D ** -0.5, 0.15625, ((2, 2),)),
        "out_weight": centred(key_of[3], (D, D), D ** -0.5, 0.15625, ((0, 2),)),
    }


def one_patch(query, key, value, grad_attn):
    scale = HEAD_DIM ** -0.5
    qf = query.astype(jnp.float32)
    kf = key.astype(jnp.float32)
    vf = value.astype(jnp.float32)
    gf = grad_attn.astype(jnp.float32)
    scores = jnp.einsum('ihe,jhe->hij', qf, kf) * scale
    peak = jnp.max(scores, axis=-1, keepdims=True)
    expo = jnp.exp(scores - peak)
    prob = expo / jnp.sum(expo, axis=-1, keepdims=True)
    weights = prob.astype(jnp.bfloat16).astype(jnp.float32)
    attn = jnp.einsum('hij,jhe->ihe', weights, vf).astype(jnp.bfloat16)
    dweights = jnp.einsum('ihe,jhe->hij', gf, vf)
    dscores = (prob * (dweights - jnp.sum(prob * dweights, axis=-1, keepdims=True)) * scale).astype(jnp.bfloat16).astype(jnp.float32)
    dvalue = jnp.einsum('hij,ihe->jhe', weights, gf).astype(jnp.bfloat16)
    dquery = jnp.einsum('hij,jhe->ihe', dscores, kf).astype(jnp.bfloat16)
    dkey = jnp.einsum('hij,ihe->jhe', dscores, qf).astype(jnp.bfloat16)
    return attn, dquery, dkey, dvalue


def reference(hidden, out_cotangent, qkv_weight, out_weight):
    flat_w = qkv_weight.reshape(D, 3 * D)
    qkv = jnp.dot(hidden, flat_w, preferred_element_type=jnp.float32).astype(jnp.bfloat16)
    grad_attn = jnp.dot(out_cotangent, out_weight.T, preferred_element_type=jnp.float32).astype(jnp.bfloat16)

    def split(values):
        return values.reshape(FRAMES, P_SIZE, HEADS, HEAD_DIM).transpose(1, 0, 2, 3)

    def join(values):
        return values.transpose(1, 0, 2, 3).reshape(TOKENS, D)

    pieces = (split(qkv[:, :D]), split(qkv[:, D:2 * D]), split(qkv[:, 2 * D:]), split(grad_attn))
    attn, dquery, dkey, dvalue = lax.map(lambda group: one_patch(*group), pieces)
    attn_rows = join(attn)
    dqkv = jnp.concatenate([join(dquery), join(dkey), join(dvalue)], axis=1)
    grad_hidden = jnp.dot(dqkv, flat_w.T, preferred_element_type=jnp.float32).astype(jnp.bfloat16)
    qkv_grad = jnp.dot(hidden.T, dqkv, preferred_element_type=jnp.float32).reshape(D, 3, D)
    out_grad = jnp.dot(attn_rows.T, out_cotangent, preferred_element_type=jnp.float32)
    return grad_hidden, qkv_grad, out_grad
```

```python
import functools

import jax
import jax.numpy as jnp
from jax import lax
from jax.experimental import pallas as pl
from jax.experimental.pallas import tpu as pltpu
from jax.sharding import PartitionSpec as P

HEAD_DIM = 88
P_SIZE = 256
MIB = 1024 * 1024
BF = jnp.bfloat16
F32 = jnp.float32
NN = (((1,), (0,)), ((), ()))
NT = (((1,), (1,)), ((), ()))
TN = (((0,), (0,)), ((), ()))


def mm(a, b, dims=NN):
    return lax.dot_general(a, b, dims, preferred_element_type=F32)


def onehot(rows, cols, match):
    r = lax.broadcasted_iota(jnp.int32, (rows, cols), 0)
    c = lax.broadcasted_iota(jnp.int32, (rows, cols), 1)
    return jnp.where(match(r, c), 1.0, 0.0).astype(BF)


def params(mib):
    return pltpu.CompilerParams(vmem_limit_bytes=mib * MIB)


def pack_kernel(x_ref, o_ref):
    width = x_ref.shape[2]
    perm = onehot(
        256,
        256,
        lambda r, c: ((r >> 4) == ((c >> 2) & 15)) & (((r >> 2) & 3) == (c & 3)) & ((r & 3) == (c >> 6)),
    )
    o_ref[...] = mm(perm, x_ref[...].reshape(256, width)).astype(BF)


def pack(x):
    tokens, width = x.shape
    return pl.pallas_call(
        pack_kernel,
        grid=(4,),
        in_specs=[pl.BlockSpec((4, 64, width), lambda b: (0, b, 0))],
        out_specs=pl.BlockSpec((256, width), lambda b: (b, 0)),
        out_shape=jax.ShapeDtypeStruct((tokens, width), BF),
        compiler_params=params(16),
        cost_estimate=pl.CostEstimate(flops=2 * tokens * 256 * width, bytes_accessed=4 * tokens * width, transcendentals=0),
        name="pack_rows",
    )(x.reshape(4, P_SIZE, width))


def by_patch(x_ref, sorted_ref):
    perm = onehot(
        256,
        256,
        lambda r, c: ((r >> 6) == ((c >> 2) & 3)) & (((r >> 2) & 15) == (c >> 4)) & ((r & 3) == (c & 3)),
    )
    for b in range(4):
        part = mm(perm, x_ref[b * 256 : (b + 1) * 256, :]).astype(BF)
        for p in range(4):
            sorted_ref[p, b * 64 : (b + 1) * 64, :] = part[p * 64 : (p + 1) * 64, :]


def forward_kernel(x_ref, w_ref, xt_ref, qkv_ref, prob_ref, attn_ref, sorted_ref):
    heads = qkv_ref.shape[1] // 3
    local = heads * HEAD_DIM
    scale = HEAD_DIM ** -0.5

    @pl.when(pl.program_id(0) == 0)
    def _():
        by_patch(x_ref, sorted_ref)

    xt = sorted_ref[pl.program_id(0)].T
    xt_ref[...] = xt
    for j in range(3):
        part = mm(w_ref[j * local : (j + 1) * local, :], xt)
        qkv_ref[0, j * heads : (j + 1) * heads] = part.reshape(heads, HEAD_DIM, 256).astype(BF)
    for h in range(heads):
        query = qkv_ref[0, h]
        key = qkv_ref[0, heads + h]
        value = qkv_ref[0, 2 * heads + h]
        scores = mm(key.T, query) * scale
        expo = jnp.exp(scores - jnp.max(scores, axis=0, keepdims=True))
        prob = expo / jnp.sum(expo, axis=0, keepdims=True)
        prob_ref[0, h] = prob
        attn_ref[0, h] = mm(value, prob.astype(BF)).astype(BF)


def forward(x, w):
    tokens, width = x.shape
    heads = w.shape[0] // 3 // HEAD_DIM
    return pl.pallas_call(
        forward_kernel,
        grid=(4,),
        in_specs=[
            pl.BlockSpec((tokens, width), lambda p: (0, 0)),
            pl.BlockSpec(w.shape, lambda p: (0, 0)),
        ],
        out_specs=[
            pl.BlockSpec((width, 256), lambda p: (0, p)),
            pl.BlockSpec((1, 3 * heads, HEAD_DIM, 256), lambda p: (p, 0, 0, 0)),
            pl.BlockSpec((1, heads, 256, 256), lambda p: (p, 0, 0, 0)),
            pl.BlockSpec((1, heads, HEAD_DIM, 256), lambda p: (p, 0, 0, 0)),
        ],
        out_shape=[
            jax.ShapeDtypeStruct((width, tokens), BF),
            jax.ShapeDtypeStruct((4, 3 * heads, HEAD_DIM, 256), BF),
            jax.ShapeDtypeStruct((4, heads, 256, 256), F32),
            jax.ShapeDtypeStruct((4, heads, HEAD_DIM, 256), BF),
        ],
        scratch_shapes=[pltpu.VMEM((4, 256, width), BF)],
        compiler_params=params(48),
        cost_estimate=pl.CostEstimate(flops=9 * 10**9, bytes_accessed=24 * 10**6, transcendentals=4 * heads * 65536),
        name="forward",
    )(x, w)


def backward_kernel(c_ref, wo_ref, w_ref, qkv_ref, prob_ref, sorted_ref, dqkv_ref, send_ref, grad_ref, cotangent_ref, total_ref):
    heads = prob_ref.shape[1]
    local = heads * HEAD_DIM
    scale = HEAD_DIM ** -0.5
    p = pl.program_id(0)

    @pl.when(p == 0)
    def _():
        by_patch(c_ref, sorted_ref)

    grad = mm(wo_ref[...], sorted_ref[p], NT)
    grad_ref[...] = grad.reshape(heads, HEAD_DIM, 256).astype(BF)
    for h in range(heads):
        query = qkv_ref[0, h]
        key = qkv_ref[0, heads + h]
        value = qkv_ref[0, 2 * heads + h]
        gout = grad_ref[h]
        prob = prob_ref[0, h]
        dvalue = mm(gout, prob.astype(BF), NT)
        dweights = mm(value.T, gout)
        mean = jnp.sum(prob * dweights, axis=0, keepdims=True)
        dscores = (prob * (dweights - mean) * scale).astype(BF)
        dquery = mm(key, dscores)
        dkey = mm(query, dscores, NT)
        cotangent_ref[h] = dquery.astype(BF)
        cotangent_ref[heads + h] = dkey.astype(BF)
        cotangent_ref[2 * heads + h] = dvalue.astype(BF)
    dqkv = cotangent_ref[...].astype(F32).reshape(3 * local, 256).astype(BF)
    dqkv_ref[...] = dqkv
    total_ref[p] = mm(w_ref[...], dqkv).astype(BF)

    @pl.when(p == 3)
    def _():
        perm = onehot(
            512,
            512,
            lambda r, c: (((r >> 2) & 3) == (c >> 7)) & ((r >> 4) == ((c >> 2) & 31)) & ((r & 3) == (c & 3)),
        )
        half = total_ref.shape[1] // 2
        for b in range(2):
            for t in range(2):
                cols = jnp.concatenate(
                    [total_ref[q, t * half : (t + 1) * half, b * 128 : (b + 1) * 128] for q in range(4)], axis=1
                )
                part = mm(perm, cols, NT).astype(BF)
                send_ref[b * 32 : (b + 1) * 32, t] = part.reshape(32, 16, half)


def backward(cot, wo, w, qkv, prob):
    tokens, width = cot.shape
    heads = prob.shape[1]
    local = heads * HEAD_DIM
    return pl.pallas_call(
        backward_kernel,
        grid=(4,),
        in_specs=[
            pl.BlockSpec((tokens, width), lambda p: (0, 0)),
            pl.BlockSpec(wo.shape, lambda p: (0, 0)),
            pl.BlockSpec(w.shape, lambda p: (0, 0)),
            pl.BlockSpec((1, 3 * heads, HEAD_DIM, 256), lambda p: (p, 0, 0, 0)),
            pl.BlockSpec((1, heads, 256, 256), lambda p: (p, 0, 0, 0)),
        ],
        out_specs=[
            pl.BlockSpec((4, 256, width), lambda p: (0, 0, 0)),
            pl.BlockSpec((3 * local, 256), lambda p: (0, p)),
            pl.BlockSpec((64, 2, 16, width // 2), lambda p: (0, 0, 0, 0)),
        ],
        out_shape=[
            jax.ShapeDtypeStruct((4, 256, width), BF),
            jax.ShapeDtypeStruct((3 * local, tokens), BF),
            jax.ShapeDtypeStruct((64, 2, 16, width // 2), BF),
        ],
        scratch_shapes=[
            pltpu.VMEM((heads, HEAD_DIM, 256), BF),
            pltpu.VMEM((3 * heads, HEAD_DIM, 256), BF),
            pltpu.VMEM((4, width, 256), BF),
        ],
        compiler_params=params(56),
        cost_estimate=pl.CostEstimate(flops=12 * 10**9, bytes_accessed=30 * 10**6, transcendentals=0),
        name="backward",
    )(cot, wo, w, qkv, prob)


def weights_kernel(core_ref, xt_ref, dqkv_ref, attn_ref, c_ref, o_ref):
    core = core_ref[0]
    width = xt_ref.shape[0]
    local = attn_ref.shape[0]
    cols = dqkv_ref.shape[0]
    step = pl.program_id(0)
    rows = o_ref.shape[0] * 24

    def device_row(r):
        place = r // 24
        return place, r - place * 24

    r = lax.broadcasted_iota(jnp.int32, (rows, width), 0) + step * rows
    place, at = device_row(r)
    f = lax.broadcasted_iota(jnp.int32, (rows, width), 1)
    pick = jnp.where((f == (2 * place + core) * 22 + at) & (at < 22), 1.0, 0.0).astype(BF)
    left = mm(pick, xt_ref[...]).astype(BF)
    o_ref[:, :, :cols] = mm(left, dqkv_ref[...], NT).astype(BF).reshape(rows // 24, 24, cols)
    r = lax.broadcasted_iota(jnp.int32, (rows, local), 0) + step * rows
    place, at = device_row(r)
    c = lax.broadcasted_iota(jnp.int32, (rows, local), 1)
    first = (2 * place + core) * 11
    low = jnp.where((c == first + at) & (at < 11), 1.0, 0.0).astype(BF)
    high = jnp.where((c == first + at - 11) & (at >= 11) & (at < 22), 1.0, 0.0).astype(BF)
    half = width // 2
    total = mm(mm(low, attn_ref[...]).astype(BF), c_ref[:, :half])
    total += mm(mm(high, attn_ref[...]).astype(BF), c_ref[:, half:])
    o_ref[:, :, cols:] = total.astype(BF).reshape(rows // 24, 24, half)


def weight_grads(core, xt, dqkv, attn, cot):
    width, tokens = xt.shape
    cols = dqkv.shape[0]
    local = attn.shape[0]
    whole = lambda a: pl.BlockSpec(a.shape, lambda s: (0,) * a.ndim)
    return pl.pallas_call(
        weights_kernel,
        grid=(4,),
        in_specs=[pl.BlockSpec(memory_space=pltpu.SMEM), whole(xt), whole(dqkv), whole(attn), whole(cot)],
        out_specs=pl.BlockSpec((8, 24, cols + width // 2), lambda s: (s, 0, 0)),
        out_shape=jax.ShapeDtypeStruct((32, 24, cols + width // 2), BF),
        compiler_params=params(56),
        cost_estimate=pl.CostEstimate(flops=8 * 10**9, bytes_accessed=24 * 10**6, transcendentals=0),
        name="weight_grads",
    )(core, xt, dqkv, attn, cot)


def unpack_kernel(x_ref, o_ref):
    half = x_ref.shape[2]
    pick = onehot(
        1024,
        512,
        lambda r, c: ((r & 3) == (c >> 7)) & ((r >> 5) == ((c >> 2) & 31)) & (((r >> 2) & 3) == (c & 3)),
    )
    for b in range(2):
        rows = x_ref[b * 64 : (b + 1) * 64].reshape(1024, half)
        part = mm(rows.T, pick).astype(BF)
        for f in range(4):
            o_ref[:, f * 256 + b * 128 : f * 256 + (b + 1) * 128] = part[:, f * 128 : (f + 1) * 128]


def unpack(x):
    half = x.shape[2]
    return pl.pallas_call(
        unpack_kernel,
        out_shape=jax.ShapeDtypeStruct((half, 1024), BF),
        compiler_params=params(32),
        cost_estimate=pl.CostEstimate(flops=2 * half * 1024 * 1024, bytes_accessed=5 * 10**6, transcendentals=0),
        name="unpack_rows",
    )(x)


def shards(hidden, out_cotangent, qkv_weight, out_weight):
    tokens, width = hidden.shape
    local = qkv_weight.shape[2]
    n_seq = lax.axis_size("seq")
    w_rows = qkv_weight.transpose(1, 2, 0).reshape(3 * local, width)
    w_cols = qkv_weight.reshape(width, 3 * local)

    def to_patches(rows):
        return lax.all_to_all(rows.reshape(n_seq, 16, width), "seq", split_axis=0, concat_axis=0, tiled=True).reshape(tokens, width)

    hidden_in = to_patches(pack(hidden))
    cot_send = pack(out_cotangent)
    hidden_in, cot_send, w_cols = lax.optimization_barrier((hidden_in, cot_send, w_cols))
    cot_in = to_patches(cot_send)
    xt, qkv, prob, attn = forward(hidden_in, w_rows)
    cot_rows, dqkv, send = backward(cot_in, out_weight, w_cols, qkv, prob)
    attn = attn.transpose(1, 2, 0, 3).reshape(local, tokens)
    cot_rows = cot_rows.reshape(tokens, width)

    returned = lax.all_to_all(send.reshape(2 * n_seq, 16, width // 2), ("seq", "tp"), split_axis=0, concat_axis=0, tiled=True)
    core = lax.axis_index("seq") % 2
    grads = functools.partial(weight_grads, xt=xt, dqkv=dqkv, attn=attn, cot=cot_rows)
    other = grads((1 - core).reshape(1).astype(jnp.int32))
    arrived = lax.ppermute(other, "seq", [(i, i ^ 1) for i in range(n_seq)])
    mine = grads(core.reshape(1).astype(jnp.int32))
    chip = (mine.astype(F32) + arrived.astype(F32)).astype(BF)
    returned, chip = lax.optimization_barrier((returned, chip))
    groups = [list(range(0, n_seq, 2)), list(range(1, n_seq, 2))]
    terms = lax.all_to_all(chip, "seq", split_axis=0, concat_axis=0, tiled=True, axis_index_groups=groups)
    grad_hidden = unpack(returned).T
    total = terms.astype(F32).sum(0)
    qkv_grad = total[:22, : 3 * local].reshape(22, 3, local)
    out_grad = total[:22, 3 * local :].reshape(2, 11, width // 2).transpose(1, 0, 2).reshape(11, width)
    return (grad_hidden, qkv_grad, out_grad)


def solution(mesh):
    return jax.shard_map(
        shards,
        mesh=mesh,
        in_specs=(P("seq", None), P("seq", None), P(None, None, "tp"), P("tp", None)),
        out_specs=(P("seq", "tp"), P("seq", None, "tp"), P(("tp", "seq"), None)),
        check_vma=False,
    )
```

```python
import functools

import jax
import jax.numpy as jnp
from jax import lax
from jax.experimental import pallas as pl
from jax.experimental.pallas import tpu as pltpu
from jax.sharding import PartitionSpec as P

HEAD_DIM = 88
P_SIZE = 256
MIB = 1024 * 1024
BF = jnp.bfloat16
F32 = jnp.float32
NN = (((1,), (0,)), ((), ()))
NT = (((1,), (1,)), ((), ()))
TN = (((0,), (0,)), ((), ()))


def mm(a, b, dims=NN):
    return lax.dot_general(a, b, dims, preferred_element_type=F32)


def onehot(rows, cols, match):
    r = lax.broadcasted_iota(jnp.int32, (rows, cols), 0)
    c = lax.broadcasted_iota(jnp.int32, (rows, cols), 1)
    return jnp.where(match(r, c), 1.0, 0.0).astype(BF)


def params(mib):
    return pltpu.CompilerParams(vmem_limit_bytes=mib * MIB)


def pack_kernel(x_ref, o_ref):
    width = x_ref.shape[2]
    perm = onehot(
        256,
        256,
        lambda r, c: ((r >> 4) == ((c >> 2) & 15)) & (((r >> 2) & 3) == (c & 3)) & ((r & 3) == (c >> 6)),
    )
    o_ref[...] = mm(perm, x_ref[...].reshape(256, width)).astype(BF)


def pack(x):
    tokens, width = x.shape
    return pl.pallas_call(
        pack_kernel,
        grid=(4,),
        in_specs=[pl.BlockSpec((4, 64, width), lambda b: (0, b, 0))],
        out_specs=pl.BlockSpec((256, width), lambda b: (b, 0)),
        out_shape=jax.ShapeDtypeStruct((tokens, width), BF),
        compiler_params=params(16),
        cost_estimate=pl.CostEstimate(flops=2 * tokens * 256 * width, bytes_accessed=4 * tokens * width, transcendentals=0),
        name="pack_rows",
    )(x.reshape(4, P_SIZE, width))


def by_patch(x_ref, sorted_ref):
    perm = onehot(
        256,
        256,
        lambda r, c: ((r >> 6) == ((c >> 2) & 3)) & (((r >> 2) & 15) == (c >> 4)) & ((r & 3) == (c & 3)),
    )
    for b in range(4):
        part = mm(perm, x_ref[b * 256 : (b + 1) * 256, :]).astype(BF)
        for p in range(4):
            sorted_ref[p, b * 64 : (b + 1) * 64, :] = part[p * 64 : (p + 1) * 64, :]


def turn_kernel(w_ref, wo_ref, halves_ref, turned_ref):
    half = halves_ref.shape[2]
    halves_ref[0] = w_ref[:, :half]
    halves_ref[1] = w_ref[:, half:]

    @pl.when(pl.program_id(0) == 0)
    def _():
        turned_ref[...] = wo_ref[...].T


def turn_weights(w, wo):
    cols, width = w.shape
    local = wo.shape[0]
    return pl.pallas_call(
        turn_kernel,
        grid=(3,),
        in_specs=[pl.BlockSpec((cols // 3, width), lambda j: (j, 0)), pl.BlockSpec(wo.shape, lambda j: (0, 0))],
        out_specs=[
            pl.BlockSpec((2, cols // 3, width // 2), lambda j: (0, j, 0)),
            pl.BlockSpec((width, local), lambda j: (0, 0)),
        ],
        out_shape=[jax.ShapeDtypeStruct((2, cols, width // 2), BF), jax.ShapeDtypeStruct((width, local), BF)],
        compiler_params=params(56),
        cost_estimate=pl.CostEstimate(flops=0, bytes_accessed=16 * 10**6, transcendentals=0),
        name="turn_weights",
    )(w, wo)


def spread(from_ref, to_ref, rows, offset):
    for core in range(2):
        for place in range(32):
            device = 2 * place + core
            to_ref[(core * 32 + place) * 24 + offset : (core * 32 + place) * 24 + offset + rows, :] = from_ref[
                device * rows : (device + 1) * rows, :
            ]


def forward_kernel(
    x_ref, w_ref, xt_ref, qkv_ref, prob_ref, attn_ref, sorted_ref, heads_ref, turned_ref, wide_ref, part_ref, low_ref, high_ref
):
    heads = qkv_ref.shape[1] // 3
    local = heads * HEAD_DIM
    scale = HEAD_DIM ** -0.5
    p = pl.program_id(0)

    @pl.when(p == 0)
    def _():
        by_patch(x_ref, sorted_ref)
        wide_ref[...] = jnp.zeros_like(wide_ref)

    xt = sorted_ref[p].T
    for j in range(3):
        part = mm(w_ref[j * local : (j + 1) * local, :], xt)
        qkv_ref[0, j * heads : (j + 1) * heads] = part.reshape(heads, HEAD_DIM, 256).astype(BF)
    turned_ref[...] = x_ref[pl.ds(pl.multiple_of(p * 256, 256), 256), :].T.astype(F32)
    spread(turned_ref, wide_ref, 22, 0)
    xt_ref[...] = wide_ref[...].astype(BF).reshape(xt_ref.shape)
    for h in range(heads):
        query = qkv_ref[0, h]
        key = qkv_ref[0, heads + h]
        value = qkv_ref[0, 2 * heads + h]
        scores = mm(key.T, query) * scale
        expo = jnp.exp(scores - jnp.max(scores, axis=0, keepdims=True))
        prob = expo / jnp.sum(expo, axis=0, keepdims=True)
        prob_ref[0, h] = prob
        heads_ref[p, h * HEAD_DIM : (h + 1) * HEAD_DIM, :] = mm(value, prob.astype(BF))

    @pl.when(p == 3)
    def _():
        low_ref[...] = jnp.zeros_like(low_ref)
        high_ref[...] = jnp.zeros_like(high_ref)
        perm = onehot(
            512,
            512,
            lambda r, c: ((r >> 7) == ((c >> 2) & 3)) & (((r >> 2) & 31) == (c >> 4)) & ((r & 3) == (c & 3)),
        )
        for b in range(2):
            cols = jnp.concatenate([heads_ref[q, :, b * 128 : (b + 1) * 128] for q in range(4)], axis=1)
            part_ref[...] = mm(cols.astype(BF), perm)
            spread(part_ref, low_ref, 11, 0)
            spread(part_ref, high_ref, 11, 11)
            rows = attn_ref.shape[1]
            attn_ref[:, :, b * 512 : (b + 1) * 512] = low_ref[...].astype(BF).reshape(2, rows, 512)
            attn_ref[:, :, 1024 + b * 512 : 1024 + (b + 1) * 512] = high_ref[...].astype(BF).reshape(2, rows, 512)


def forward(x, w):
    tokens, width = x.shape
    heads = w.shape[0] // 3 // HEAD_DIM
    local = heads * HEAD_DIM
    once = pl.Buffered(buffer_count=1)
    return pl.pallas_call(
        forward_kernel,
        grid=(4,),
        in_specs=[
            pl.BlockSpec((tokens, width), lambda p: (0, 0), pipeline_mode=once),
            pl.BlockSpec(w.shape, lambda p: (0, 0), pipeline_mode=once),
        ],
        out_specs=[
            pl.BlockSpec((2, 768, 256), lambda p: (0, 0, p)),
            pl.BlockSpec((1, 3 * heads, HEAD_DIM, 256), lambda p: (p, 0, 0, 0)),
            pl.BlockSpec((1, heads, 256, 256), lambda p: (p, 0, 0, 0)),
            pl.BlockSpec((2, 768, 2 * tokens), lambda p: (0, 0, 0)),
        ],
        out_shape=[
            jax.ShapeDtypeStruct((2, 768, tokens), BF),
            jax.ShapeDtypeStruct((4, 3 * heads, HEAD_DIM, 256), BF),
            jax.ShapeDtypeStruct((4, heads, 256, 256), F32),
            jax.ShapeDtypeStruct((2, 768, 2 * tokens), BF),
        ],
        scratch_shapes=[
            pltpu.VMEM((4, 256, width), BF),
            pltpu.VMEM((4, local, 256), F32),
            pltpu.VMEM((width, 256), F32),
            pltpu.VMEM((1536, 256), F32),
            pltpu.VMEM((local, 512), F32),
            pltpu.VMEM((1536, 512), F32),
            pltpu.VMEM((1536, 512), F32),
        ],
        compiler_params=params(60),
        cost_estimate=pl.CostEstimate(flops=9 * 10**9, bytes_accessed=24 * 10**6, transcendentals=4 * heads * 65536),
        name="forward",
    )(x, w)


def backward_kernel(
    c_ref, wo_ref, w_any, qkv_ref, prob_ref, dqkv_ref, send_ref, sorted_ref, grad_ref, terms_ref, patch_ref, w_ref, sem
):
    heads = prob_ref.shape[1]
    local = heads * HEAD_DIM
    scale = HEAD_DIM ** -0.5
    p = pl.program_id(0)
    weights = pltpu.make_async_copy(w_any, w_ref, sem)

    @pl.when(p == 0)
    def _():
        weights.start()
        terms_ref[...] = mm(c_ref[...], wo_ref[...])
        perm = onehot(
            256,
            256,
            lambda r, c: ((r >> 6) == ((c >> 2) & 3)) & (((r >> 2) & 15) == (c >> 4)) & ((r & 3) == (c & 3)),
        )
        for b in range(4):
            part = mm(perm, terms_ref[b * 256 : (b + 1) * 256, :].astype(BF)).astype(BF)
            for q in range(4):
                sorted_ref[q, b * 64 : (b + 1) * 64, :] = part[q * 64 : (q + 1) * 64, :]

    grad_ref[...] = sorted_ref[p].T.astype(F32).reshape(heads, HEAD_DIM, 256).astype(BF)
    for h in range(heads):
        query = qkv_ref[0, h]
        key = qkv_ref[0, heads + h]
        value = qkv_ref[0, 2 * heads + h]
        gout = grad_ref[h]
        prob = prob_ref[0, h]
        dvalue = mm(gout, prob.astype(BF), NT)
        dweights = mm(value.T, gout)
        mean = jnp.sum(prob * dweights, axis=0, keepdims=True)
        dscores = (prob * (dweights - mean) * scale).astype(BF)
        dquery = mm(key, dscores)
        dkey = mm(query, dscores, NT)
        for j, value in enumerate((dquery, dkey, dvalue)):
            at = j * local + h * HEAD_DIM
            patch_ref[p, at : at + HEAD_DIM, :] = value

    @pl.when(p == 3)
    def _():
        weights.wait()
        perm = onehot(
            256,
            256,
            lambda r, c: ((c >> 6) == ((r >> 2) & 3)) & (((c >> 2) & 15) == (r >> 4)) & ((r & 3) == (c & 3)),
        )
        turned = [patch_ref[q].astype(BF).T for q in range(4)]
        for b in range(4):
            rows = jnp.concatenate([turned[q][b * 64 : (b + 1) * 64, :] for q in range(4)], axis=0)
            dqkv_ref[b * 256 : (b + 1) * 256, :] = mm(perm, rows).astype(BF)
        for t in range(2):
            terms_ref[...] = mm(dqkv_ref[...], w_ref[t])
            send_ref[:, t] = terms_ref[...].astype(BF).reshape(64, 16, terms_ref.shape[1])


def backward(cot, wo, w, qkv, prob):
    tokens, width = cot.shape
    heads = prob.shape[1]
    local = heads * HEAD_DIM
    once = pl.Buffered(buffer_count=1)
    return pl.pallas_call(
        backward_kernel,
        grid=(4,),
        in_specs=[
            pl.BlockSpec((tokens, width), lambda p: (0, 0), pipeline_mode=once),
            pl.BlockSpec(wo.shape, lambda p: (0, 0), pipeline_mode=once),
            pl.BlockSpec(memory_space=pl.ANY),
            pl.BlockSpec((1, 3 * heads, HEAD_DIM, 256), lambda p: (p, 0, 0, 0)),
            pl.BlockSpec((1, heads, 256, 256), lambda p: (p, 0, 0, 0)),
        ],
        out_specs=[
            pl.BlockSpec((tokens, 3 * local), lambda p: (0, 0)),
            pl.BlockSpec((64, 2, 16, width // 2), lambda p: (0, 0, 0, 0)),
        ],
        out_shape=[
            jax.ShapeDtypeStruct((tokens, 3 * local), BF),
            jax.ShapeDtypeStruct((64, 2, 16, width // 2), BF),
        ],
        scratch_shapes=[
            pltpu.VMEM((4, 256, local), BF),
            pltpu.VMEM((heads, HEAD_DIM, 256), BF),
            pltpu.VMEM((tokens, local), F32),
            pltpu.VMEM((4, 3 * local, 256), F32),
            pltpu.VMEM(w.shape, BF),
            pltpu.SemaphoreType.DMA,
        ],
        compiler_params=params(60),
        cost_estimate=pl.CostEstimate(flops=12 * 10**9, bytes_accessed=30 * 10**6, transcendentals=0),
        name="backward",
    )(cot, wo, w, qkv, prob)


def weights_kernel(core_ref, xt_ref, dqkv_ref, attn_ref, c_ref, o_ref, halves_ref):
    tokens, cols = dqkv_ref.shape
    half = c_ref.shape[1] // 2
    places = o_ref.shape[0]

    @pl.when(pl.program_id(0) == 0)
    def _():
        halves_ref[:tokens] = c_ref[:, :half]
        halves_ref[tokens:] = c_ref[:, half:]

    o_ref[:, :, :cols] = mm(xt_ref[0], dqkv_ref[...]).astype(BF).reshape(places, 24, cols)
    o_ref[:, :, cols:] = mm(attn_ref[0], halves_ref[...]).astype(BF).reshape(places, 24, half)


def weight_grads(core, xt, dqkv, attn, cot):
    tokens, cols = dqkv.shape
    half = cot.shape[1] // 2
    once = pl.Buffered(buffer_count=1)
    return pl.pallas_call(
        weights_kernel,
        grid_spec=pltpu.PrefetchScalarGridSpec(
            num_scalar_prefetch=1,
            grid=(2,),
            in_specs=[
                pl.BlockSpec((1, 384, tokens), lambda s, core: (core[0], s, 0)),
                pl.BlockSpec(dqkv.shape, lambda s, core: (0, 0), pipeline_mode=once),
                pl.BlockSpec((1, 384, 2 * tokens), lambda s, core: (core[0], s, 0)),
                pl.BlockSpec(cot.shape, lambda s, core: (0, 0), pipeline_mode=once),
            ],
            out_specs=pl.BlockSpec((16, 24, cols + half), lambda s, core: (s, 0, 0)),
            scratch_shapes=[pltpu.VMEM((2 * tokens, half), BF)],
        ),
        out_shape=jax.ShapeDtypeStruct((32, 24, cols + half), BF),
        compiler_params=params(56),
        cost_estimate=pl.CostEstimate(flops=6 * 10**9, bytes_accessed=18 * 10**6, transcendentals=0),
        name="weight_grads",
    )(core, xt, dqkv, attn, cot)


def split_kernel(at_ref, *refs, n_terms):
    k = pl.program_id(0)
    low, high, outs = refs[:n_terms], refs[n_terms : 2 * n_terms], refs[2 * n_terms :]
    for group, terms in ((0, low), (1, high)):
        total = terms[0][...].astype(F32)
        for term in terms[1:]:
            total += term[...].astype(F32)
        for q in range(4):

            @pl.when(k == q)
            def _():
                outs[4 * group + q][...] = total.astype(BF).reshape(outs[q].shape)


def split_sum(at, lows, highs, low_spec, high_spec, shape, name):
    n_terms = len(lows)
    whole = pl.BlockSpec(shape, lambda k, at: (0,) * len(shape))
    return pl.pallas_call(
        functools.partial(split_kernel, n_terms=n_terms),
        grid_spec=pltpu.PrefetchScalarGridSpec(
            num_scalar_prefetch=1,
            grid=(4,),
            in_specs=[low_spec] * n_terms + [high_spec] * n_terms,
            out_specs=[whole] * 8,
        ),
        out_shape=[jax.ShapeDtypeStruct(shape, BF)] * 8,
        compiler_params=params(40),
        cost_estimate=pl.CostEstimate(flops=10**6, bytes_accessed=10 * shape[0] * shape[-1] * 24, transcendentals=0),
        name=name,
    )(at, *lows, *highs)


def pair_kernel(at_ref, *refs):
    mine_ref, other_ref = refs[8:]
    for group in range(2):
        total = refs[4 * group][...].astype(F32)
        for term in refs[4 * group + 1 : 4 * group + 4]:
            total += term[...].astype(F32)
        z = at_ref[2]
        mine_ref[group] = jnp.where(z == 0, total[0], total[1])
        other_ref[group] = jnp.where(z == 0, total[1], total[0]).astype(BF)


def pair_sum(at, terms):
    shape = terms[0].shape
    return pl.pallas_call(
        pair_kernel,
        in_specs=[pl.BlockSpec(memory_space=pltpu.SMEM)] + [pl.BlockSpec(memory_space=pltpu.VMEM)] * 8,
        out_shape=[jax.ShapeDtypeStruct(shape, F32), jax.ShapeDtypeStruct(shape, BF)],
        compiler_params=params(16),
        name="pair_sum",
    )(at, *terms)


def final_kernel(mine_ref, other_ref, qkv_ref, out_ref):
    half = out_ref.shape[1] // 2
    low = mine_ref[0] + other_ref[0].astype(F32)
    high = mine_ref[1] + other_ref[1].astype(F32)
    qkv_ref[0] = low[:22, :half]
    qkv_ref[1] = low[:22, half:]
    qkv_ref[2] = high[:22, :half]
    out_ref[:, :half] = high[:11, half:]
    out_ref[:, half:] = high[11:22, half:]


def final_sum(mine, other):
    width = mine.shape[2]
    return pl.pallas_call(
        final_kernel,
        out_shape=[jax.ShapeDtypeStruct((3, 22, width // 2), F32), jax.ShapeDtypeStruct((11, width), F32)],
        compiler_params=params(16),
        name="final_sum",
    )(mine, other)


def sum_over_chips(mine, arrived, at):
    width = mine.shape[1] // 2
    mine, arrived = (a.reshape(2, 4, 4, 24, 2 * width) for a in (mine, arrived))

    def to(step_x, step_y, flip=0):
        pairs = []
        for i in range(64):
            z, x, y, core = i // 32, i // 8 % 4, i // 2 % 4, i % 2
            pairs.append((i, (((z ^ flip) * 4 + (x + step_x) % 4) * 4 + (y + step_y) % 4) * 2 + core))
        return pairs

    first = split_sum(
        at,
        [mine, arrived],
        [mine, arrived],
        pl.BlockSpec((2, 1, 4, 24, width), lambda k, at: (0, (at[0] + k) % 4, 0, 0, 0)),
        pl.BlockSpec((2, 4, 1, 24, width), lambda k, at: (0, 0, (at[1] + k) % 4, 0, 1)),
        (2, 4, 24, width),
        "core_sum",
    )
    lows = [first[0]] + [lax.ppermute(first[k], "seq", to(k, 0)) for k in (1, 2, 3)]
    highs = [first[4]] + [lax.ppermute(first[4 + k], "seq", to(0, k)) for k in (1, 2, 3)]
    second = split_sum(
        at,
        lows,
        highs,
        pl.BlockSpec((2, 1, 24, width), lambda k, at: (0, (at[1] + k) % 4, 0, 0)),
        pl.BlockSpec((2, 1, 24, width), lambda k, at: (0, (at[0] + k) % 4, 0, 0)),
        (2, 24, width),
        "ring_sum",
    )
    lows = [second[0]] + [lax.ppermute(second[k], "seq", to(0, k)) for k in (1, 2, 3)]
    highs = [second[4]] + [lax.ppermute(second[4 + k], "seq", to(k, 0)) for k in (1, 2, 3)]
    kept, given = pair_sum(at, lows + highs)
    return final_sum(kept, lax.ppermute(given, "seq", to(0, 0, 1)))


def unpack_kernel(x_ref, o_ref):
    half = x_ref.shape[2]
    pick = onehot(
        1024,
        512,
        lambda r, c: ((r & 3) == (c >> 7)) & ((r >> 5) == ((c >> 2) & 31)) & (((r >> 2) & 3) == (c & 3)),
    )
    for b in range(2):
        rows = x_ref[b * 64 : (b + 1) * 64].reshape(1024, half)
        part = mm(rows.T, pick).astype(BF)
        for f in range(4):
            o_ref[:, f * 256 + b * 128 : f * 256 + (b + 1) * 128] = part[:, f * 128 : (f + 1) * 128]


def unpack(x):
    half = x.shape[2]
    return pl.pallas_call(
        unpack_kernel,
        out_shape=jax.ShapeDtypeStruct((half, 1024), BF),
        compiler_params=params(32),
        cost_estimate=pl.CostEstimate(flops=2 * half * 1024 * 1024, bytes_accessed=5 * 10**6, transcendentals=0),
        name="unpack_rows",
    )(x)


def shards(hidden, out_cotangent, qkv_weight, out_weight):
    tokens, width = hidden.shape
    local = qkv_weight.shape[2]
    n_seq = lax.axis_size("seq")
    w_rows = qkv_weight.transpose(1, 2, 0).reshape(3 * local, width)
    w_halves, wo_turned = turn_weights(w_rows, out_weight)

    def to_patches(rows):
        return lax.all_to_all(rows.reshape(n_seq, 16, width), "seq", split_axis=0, concat_axis=0, tiled=True).reshape(tokens, width)

    hidden_in = to_patches(pack(hidden))
    cot_send = pack(out_cotangent)
    hidden_in, cot_send, w_halves, wo_turned = lax.optimization_barrier((hidden_in, cot_send, w_halves, wo_turned))
    cot_in = to_patches(cot_send)
    xt, qkv, prob, attn = forward(hidden_in, w_rows)
    dqkv, send = backward(cot_in, wo_turned, w_halves, qkv, prob)

    returned = lax.all_to_all(send.reshape(2 * n_seq, 16, width // 2), ("seq", "tp"), split_axis=0, concat_axis=0, tiled=True)
    place = lax.axis_index("seq").astype(jnp.int32)
    core = place % 2
    at = jnp.stack([place // 8 % 4, place // 2 % 4, place // 32])
    grads = functools.partial(weight_grads, xt=xt, dqkv=dqkv, attn=attn, cot=cot_in)
    other = grads((1 - core).reshape(1))
    arrived = lax.ppermute(other, "seq", [(i, i ^ 1) for i in range(n_seq)])
    mine = grads(core.reshape(1))
    shape = (32 * 24, 3 * local + width // 2)
    qkv_grad, out_grad = sum_over_chips(mine.reshape(shape), arrived.reshape(shape), at)
    return (unpack(returned).T, qkv_grad.transpose(1, 0, 2), out_grad)


def solution(mesh):
    return jax.shard_map(
        shards,
        mesh=mesh,
        in_specs=(P("seq", None), P("seq", None), P(None, None, "tp"), P("tp", None)),
        out_specs=(P("seq", "tp"), P("seq", None, "tp"), P(("tp", "seq"), None)),
        check_vma=False,
    )
```

```python
import functools

import jax
import jax.numpy as jnp
from jax import lax
from jax.experimental import pallas as pl
from jax.experimental.pallas import tpu as pltpu
from jax.sharding import PartitionSpec as P

HEAD_DIM = 88
P_SIZE = 256
MIB = 1024 * 1024
BF = jnp.bfloat16
F32 = jnp.float32
NN = (((1,), (0,)), ((), ()))
NT = (((1,), (1,)), ((), ()))
TN = (((0,), (0,)), ((), ()))


def mm(a, b, dims=NN):
    return lax.dot_general(a, b, dims, preferred_element_type=F32)


def onehot(rows, cols, match):
    r = lax.broadcasted_iota(jnp.int32, (rows, cols), 0)
    c = lax.broadcasted_iota(jnp.int32, (rows, cols), 1)
    return jnp.where(match(r, c), 1.0, 0.0).astype(BF)


def hint(flops, size):
    return pl.CostEstimate(flops=flops, bytes_accessed=size, transcendentals=0)


def params(mib):
    return pltpu.CompilerParams(vmem_limit_bytes=mib * MIB)


def pack_kernel(x_ref, c_ref, o_ref, perm_ref):
    width = x_ref.shape[2]

    @pl.when(pl.program_id(0) == 0)
    def _():
        perm_ref[...] = onehot(
            512,
            512,
            lambda r, c: ((r >> 4) == ((c >> 1) & 31))
            & (((r >> 3) & 1) == (c >> 8))
            & (((r >> 2) & 1) == (c & 1))
            & ((r & 3) == ((c >> 6) & 3)),
        )

    rows = jnp.concatenate([x_ref[...].reshape(256, width), c_ref[...].reshape(256, width)], axis=0)
    o_ref[...] = mm(perm_ref[...], rows).astype(BF)


def pack(x, c, part):
    tokens, width = x.shape
    spec = pl.BlockSpec((4, 64, width), lambda b: (0, 2 * part + b, 0))
    return pl.pallas_call(
        pack_kernel,
        grid=(2,),
        in_specs=[spec, spec],
        out_specs=pl.BlockSpec((512, width), lambda b: (b, 0)),
        out_shape=jax.ShapeDtypeStruct((tokens, width), BF),
        scratch_shapes=[pltpu.VMEM((512, 512), BF)],
        compiler_params=params(60),
        cost_estimate=hint(10**6, 10**6),
        name="pack_rows",
    )(x.reshape(4, P_SIZE, width), c.reshape(4, P_SIZE, width))


def turn_kernel(w_ref, halves_ref):
    half = halves_ref.shape[2]
    halves_ref[0] = w_ref[:, :half]
    halves_ref[1] = w_ref[:, half:]


def turn_weights(w):
    cols, width = w.shape
    return pl.pallas_call(
        turn_kernel,
        grid=(3,),
        in_specs=[pl.BlockSpec((cols // 3, width), lambda j: (j, 0))],
        out_specs=pl.BlockSpec((2, cols // 3, width // 2), lambda j: (0, j, 0)),
        out_shape=jax.ShapeDtypeStruct((2, cols, width // 2), BF),
        compiler_params=params(60),
        cost_estimate=hint(10**6, 10**6),
        name="turn_weights",
    )(w)


def spread(from_ref, to_ref, rows, offset):
    for core in range(2):
        for place in range(32):
            device = 2 * place + core
            to_ref[core, place * 24 + offset : place * 24 + offset + rows, :] = from_ref[device * rows : (device + 1) * rows, :]


def attend_kernel(
    x_any,
    w_any,
    wo_any,
    xt_ref,
    low_ref,
    high_ref,
    dqkv_ref,
    cot_ref,
    sorted_ref,
    qkv_ref,
    grad_ref,
    turned_ref,
    wide_ref,
    attn_ref,
    upper_ref,
    lower_ref,
    patch_ref,
    x_ref,
    w_ref,
    wo_ref,
    sems,
):
    heads = grad_ref.shape[0]
    local = heads * HEAD_DIM
    scale = HEAD_DIM ** -0.5
    p = pl.program_id(0)
    copies = [
        pltpu.make_async_copy(source, target, sems.at[n])
        for n, (source, target) in enumerate(((x_any, x_ref), (w_any, w_ref), (wo_any, wo_ref)))
    ]

    @pl.when(p == 0)
    def _():
        for copy in copies:
            copy.start()
        copies[0].wait()
        perm = onehot(
            256,
            256,
            lambda r, c: ((r >> 6) == ((c >> 2) & 3)) & (((r >> 2) & 15) == (c >> 4)) & ((r & 3) == (c & 3)),
        )
        for b in range(4):
            part = mm(perm, x_ref[b * 256 : (b + 1) * 256, :]).astype(BF)
            for q in range(4):
                sorted_ref[q, b * 64 : (b + 1) * 64, :] = part[q * 64 : (q + 1) * 64, :]
        wide_ref[...] = jnp.zeros_like(wide_ref)
        upper_ref[...] = jnp.zeros_like(upper_ref)
        lower_ref[...] = jnp.zeros_like(lower_ref)
        copies[1].wait()
        copies[2].wait()

    xt = sorted_ref[p].T
    for j in range(3):
        part = mm(w_ref[j * local : (j + 1) * local, :], xt)
        qkv_ref[j * heads : (j + 1) * heads] = part.reshape(heads, HEAD_DIM, 256).astype(BF)
    cot = sorted_ref[2 + p]
    cot_ref[0] = cot
    grad_ref[...] = mm(wo_ref[...], cot.T).reshape(heads, HEAD_DIM, 256).astype(BF)
    turned_ref[...] = xt.astype(F32)
    spread(turned_ref, wide_ref, 22, 0)
    xt_ref[...] = wide_ref[...].astype(BF)
    for h in range(heads):
        query = qkv_ref[h]
        key = qkv_ref[heads + h]
        value = qkv_ref[2 * heads + h]
        gout = grad_ref[h]
        scores = mm(key.T, query) * scale
        expo = jnp.exp(scores - jnp.max(scores, axis=0, keepdims=True))
        prob = expo / jnp.sum(expo, axis=0, keepdims=True)
        weights = prob.astype(BF)
        attn_ref[h * HEAD_DIM : (h + 1) * HEAD_DIM, :] = mm(value, weights)
        dvalue = mm(gout, weights, NT)
        dweights = mm(value.T, gout)
        mean = jnp.sum(prob * dweights, axis=0, keepdims=True)
        dscores = (prob * (dweights - mean) * scale).astype(BF)
        dquery = mm(key, dscores)
        dkey = mm(query, dscores, NT)
        for j, term in enumerate((dquery, dkey, dvalue)):
            at = j * local + h * HEAD_DIM
            patch_ref[at : at + HEAD_DIM, :] = term
    dqkv_ref[0, :, : 3 * local] = patch_ref[...].astype(BF).T
    dqkv_ref[0, :, 3 * local :] = jnp.zeros((256, dqkv_ref.shape[2] - 3 * local), BF)
    spread(attn_ref, upper_ref, 11, 0)
    spread(attn_ref, lower_ref, 11, 11)
    low_ref[...] = upper_ref[...].astype(BF)
    high_ref[...] = lower_ref[...].astype(BF)


def attend(x, w, wo):
    tokens, width = x.shape
    local = wo.shape[0]
    heads = local // HEAD_DIM
    cols = -(-3 * local // 128) * 128
    spread_spec = pl.BlockSpec((2, 768, 256), lambda p: (0, 0, p))
    spread_shape = jax.ShapeDtypeStruct((2, 768, 512), BF)
    return pl.pallas_call(
        attend_kernel,
        grid=(2,),
        in_specs=[pl.BlockSpec(memory_space=pl.ANY)] * 3,
        out_specs=[
            spread_spec,
            spread_spec,
            spread_spec,
            pl.BlockSpec((1, 256, cols), lambda p: (p, 0, 0)),
            pl.BlockSpec((1, 256, width), lambda p: (p, 0, 0)),
        ],
        out_shape=[
            spread_shape,
            spread_shape,
            spread_shape,
            jax.ShapeDtypeStruct((2, 256, cols), BF),
            jax.ShapeDtypeStruct((2, 256, width), BF),
        ],
        scratch_shapes=[
            pltpu.VMEM((4, 256, width), BF),
            pltpu.VMEM((3 * heads, HEAD_DIM, 256), BF),
            pltpu.VMEM((heads, HEAD_DIM, 256), BF),
            pltpu.VMEM((width, 256), F32),
            pltpu.VMEM((2, 768, 256), F32),
            pltpu.VMEM((local, 256), F32),
            pltpu.VMEM((2, 768, 256), F32),
            pltpu.VMEM((2, 768, 256), F32),
            pltpu.VMEM((3 * local, 256), F32),
            pltpu.VMEM(x.shape, BF),
            pltpu.VMEM(w.shape, BF),
            pltpu.VMEM(wo.shape, BF),
            pltpu.SemaphoreType.DMA((3,)),
        ],
        compiler_params=params(60),
        cost_estimate=hint(10**6, 10**6),
        name="attend",
    )(x, w, wo)


def input_kernel(first_any, second_any, w_any, send_any, dqkv_ref, w_ref, rows_ref, part_ref, sems):
    cols, half = w_ref.shape[1:]
    copies = [
        pltpu.make_async_copy(source, target, sems.at[n])
        for n, (source, target) in enumerate(
            (
                (first_any, dqkv_ref.at[0:2]),
                (second_any, dqkv_ref.at[2:4]),
                (w_any.at[0], w_ref.at[0]),
                (w_any.at[1], w_ref.at[1]),
            )
        )
    ]
    for copy in copies:
        copy.start()
    perm = onehot(
        256,
        256,
        lambda r, c: ((c >> 6) == ((r >> 2) & 3)) & (((c >> 2) & 15) == (r >> 4)) & ((r & 3) == (c & 3)),
    )
    copies[0].wait()
    copies[1].wait()
    for b in range(4):
        rows = dqkv_ref[:, b * 64 : (b + 1) * 64, :cols].reshape(256, cols)
        rows_ref[b * 256 : (b + 1) * 256, :] = mm(perm, rows).astype(BF)
    outs = [pltpu.make_async_copy(part_ref.at[t], send_any.at[:, t], sems.at[4 + t]) for t in range(2)]
    for t in range(2):
        copies[2 + t].wait()
        for b in range(2):
            part = mm(rows_ref[b * 512 : (b + 1) * 512, :], w_ref[t])
            part_ref[t, b * 32 : (b + 1) * 32] = part.astype(BF).reshape(32, 16, half)
        outs[t].start()
    for out in outs:
        out.wait()


def input_grads(first, second, w):
    cols, half = w.shape[1:]
    hbm = pl.BlockSpec(memory_space=pl.ANY)
    return pl.pallas_call(
        input_kernel,
        in_specs=[hbm, hbm, hbm],
        out_specs=hbm,
        out_shape=jax.ShapeDtypeStruct((64, 2, 16, half), BF),
        scratch_shapes=[
            pltpu.VMEM((4, *first.shape[1:]), BF),
            pltpu.VMEM(w.shape, BF),
            pltpu.VMEM((1024, cols), BF),
            pltpu.VMEM((2, 64, 16, half), BF),
            pltpu.SemaphoreType.DMA((6,)),
        ],
        compiler_params=params(60),
        cost_estimate=hint(10**6, 10**6),
        name="input_grads",
    )(first, second, w)


def weights_kernel(core_ref, xt_ref, low_ref, high_ref, dqkv_ref, c_ref, *refs):
    o_ref = refs[-1]
    places = o_ref.shape[0]
    half = c_ref.shape[1] // 2
    cols = 3 * half

    def put(value, at):
        value = value.reshape(places, 24, value.shape[1])
        if len(refs) == 2:
            value += refs[0][:, :, at].astype(F32)
        o_ref[:, :, at] = value.astype(BF)

    put(mm(xt_ref[0], dqkv_ref[:, :cols]), slice(0, cols))
    put(mm(low_ref[0], c_ref[:, :half]) + mm(high_ref[0], c_ref[:, half:]), slice(cols, cols + half))


def weight_grads(core, terms, before=None, flops=10**6):
    xt, low, high, dqkv, cot = terms
    tokens = xt.shape[2]
    dqkv, cot = dqkv.reshape(tokens, -1), cot.reshape(tokens, -1)
    width = cot.shape[1]
    once = pl.Buffered(buffer_count=1)
    rows_spec = pl.BlockSpec((1, 384, tokens), lambda s, core: (core[0], s, 0))
    out_spec = pl.BlockSpec((16, 24, 2 * width), lambda s, core: (s, 0, 0))
    given = [] if before is None else [before]
    return pl.pallas_call(
        weights_kernel,
        grid_spec=pltpu.PrefetchScalarGridSpec(
            num_scalar_prefetch=1,
            grid=(2,),
            in_specs=[
                rows_spec,
                rows_spec,
                rows_spec,
                pl.BlockSpec(dqkv.shape, lambda s, core: (0, 0), pipeline_mode=once),
                pl.BlockSpec(cot.shape, lambda s, core: (0, 0), pipeline_mode=once),
            ]
            + [out_spec] * len(given),
            out_specs=out_spec,
        ),
        out_shape=jax.ShapeDtypeStruct((32, 24, 2 * width), BF),
        compiler_params=params(60),
        cost_estimate=hint(flops, 10**6),
        name="weight_grads",
    )(core, xt, low, high, dqkv, cot, *given)


def core_kernel(at_ref, mine_low, other_low, mine_high, other_high, *outs):
    k = pl.program_id(0)
    for group, terms in enumerate(((mine_low, other_low), (mine_high, other_high))):
        total = (terms[0][...].astype(F32) + terms[1][...].astype(F32)).astype(BF).reshape(outs[0].shape)
        own, after, before, left, right = outs[5 * group : 5 * group + 5]

        @pl.when(k == 0)
        def _():
            own[...] = total

        @pl.when(k == 1)
        def _():
            after[...] = total

        @pl.when(k == 3)
        def _():
            before[...] = total

        @pl.when(k == 2)
        def _():
            left[...] = total[0]
            right[...] = total[1]


def core_sum(at, mine, arrived):
    width = mine.shape[4] // 2
    shape = (2, 4, 24, width)
    low = pl.BlockSpec((2, 1, 4, 24, width), lambda k, at: (0, (at[0] + k) % 4, 0, 0, 0))
    high = pl.BlockSpec((2, 4, 1, 24, width), lambda k, at: (0, 0, (at[1] + k) % 4, 0, 1))
    shapes = ([shape] * 3 + [shape[1:]] * 2) * 2
    return pl.pallas_call(
        core_kernel,
        grid_spec=pltpu.PrefetchScalarGridSpec(
            num_scalar_prefetch=1,
            grid=(4,),
            in_specs=[low, low, high, high],
            out_specs=[pl.BlockSpec(shape, lambda k, at, n=len(shape): (0,) * n) for shape in shapes],
        ),
        out_shape=[jax.ShapeDtypeStruct(shape, BF) for shape in shapes],
        compiler_params=params(40),
        cost_estimate=hint(10**6, 10**6),
        name="core_sum",
    )(at, mine, arrived, mine, arrived)


def pass_kernel(*refs):
    ins, outs = refs[:8], refs[8:]
    for group in range(2):
        after, before, left, right = ins[4 * group : 4 * group + 4]
        outs[2 * group][0] = (after[0].astype(F32) + left[...].astype(F32)).astype(BF)
        outs[2 * group][1] = after[1]
        outs[2 * group + 1][0] = before[0]
        outs[2 * group + 1][1] = (before[1].astype(F32) + right[...].astype(F32)).astype(BF)


def pass_on(*terms):
    return pl.pallas_call(
        pass_kernel,
        out_shape=[jax.ShapeDtypeStruct(terms[0].shape, BF)] * 4,
        compiler_params=params(24),
        cost_estimate=hint(10**6, 10**6),
        name="pass_on",
    )(*terms)


def ring_kernel(at_ref, *refs):
    k = pl.program_id(0)
    outs = refs[6:]
    for group in range(2):
        total = refs[3 * group][...].astype(F32)
        for term in refs[3 * group + 1 : 3 * group + 3]:
            total += term[...].astype(F32)
        for q in range(4):

            @pl.when(k == q)
            def _():
                outs[4 * group + q][...] = total.astype(BF).reshape(outs[q].shape)


def ring_sum(at, lows, highs):
    width = lows[0].shape[3]
    shape = (2, 24, width)
    low = pl.BlockSpec((2, 1, 24, width), lambda k, at: (0, (at[1] + k) % 4, 0, 0))
    high = pl.BlockSpec((2, 1, 24, width), lambda k, at: (0, (at[0] + k) % 4, 0, 0))
    return pl.pallas_call(
        ring_kernel,
        grid_spec=pltpu.PrefetchScalarGridSpec(
            num_scalar_prefetch=1,
            grid=(4,),
            in_specs=[low] * 3 + [high] * 3,
            out_specs=[pl.BlockSpec(shape, lambda k, at: (0, 0, 0))] * 8,
        ),
        out_shape=[jax.ShapeDtypeStruct(shape, BF)] * 8,
        compiler_params=params(40),
        cost_estimate=hint(10**6, 10**6),
        name="ring_sum",
    )(at, *lows, *highs)


def pair_kernel(at_ref, *refs):
    mine_ref, other_ref = refs[8:]
    for group in range(2):
        total = refs[4 * group][...].astype(F32)
        for term in refs[4 * group + 1 : 4 * group + 4]:
            total += term[...].astype(F32)
        z = at_ref[2]
        mine_ref[group] = jnp.where(z == 0, total[0], total[1])
        other_ref[group] = jnp.where(z == 0, total[1], total[0]).astype(BF)


def pair_sum(at, terms):
    shape = terms[0].shape
    return pl.pallas_call(
        pair_kernel,
        in_specs=[pl.BlockSpec(memory_space=pltpu.SMEM)] + [pl.BlockSpec(memory_space=pltpu.VMEM)] * 8,
        out_shape=[jax.ShapeDtypeStruct(shape, F32), jax.ShapeDtypeStruct(shape, BF)],
        compiler_params=params(16),
        name="pair_sum",
    )(at, *terms)


def final_kernel(mine_ref, other_ref, qkv_ref, out_ref):
    half = out_ref.shape[1] // 2
    low = mine_ref[0] + other_ref[0].astype(F32)
    high = mine_ref[1] + other_ref[1].astype(F32)
    qkv_ref[0] = low[:22, :half]
    qkv_ref[1] = low[:22, half:]
    qkv_ref[2] = high[:22, :half]
    out_ref[:, :half] = high[:11, half:]
    out_ref[:, half:] = high[11:22, half:]


def final_sum(mine, other):
    width = mine.shape[2]
    return pl.pallas_call(
        final_kernel,
        out_shape=[jax.ShapeDtypeStruct((3, 22, width // 2), F32), jax.ShapeDtypeStruct((11, width), F32)],
        compiler_params=params(16),
        name="final_sum",
    )(mine, other)


def sum_over_chips(mine, arrived, at, beside):
    width = mine.shape[1] // 2
    mine, arrived = (a.reshape(2, 4, 4, 24, 2 * width) for a in (mine, arrived))

    def to(step_x, step_y, flip=0):
        pairs = []
        for i in range(64):
            z, x, y, core = i // 32, i // 8 % 4, i // 2 % 4, i % 2
            pairs.append((i, (((z ^ flip) * 4 + (x + step_x) % 4) * 4 + (y + step_y) % 4) * 2 + core))
        return pairs

    first = core_sum(at, mine, arrived)
    steps = ((1, 0), (-1, 0), (0, 1), (0, -1))
    halves = [lax.ppermute(first[n], "seq", to(*step)) for n, step in zip((3, 4, 8, 9), steps)]
    passed = pass_on(first[1], first[2], *halves[:2], first[6], first[7], *halves[2:])
    passed = [lax.ppermute(value, "seq", to(*step)) for value, step in zip(passed, steps)]
    second = ring_sum(at, [first[0], *passed[:2]], [first[5], *passed[2:]])
    lows = [second[0]] + [lax.ppermute(second[k], "seq", to(0, k)) for k in (1, 2, 3)]
    highs = [second[4]] + [lax.ppermute(second[4 + k], "seq", to(k, 0)) for k in (1, 2, 3)]
    kept, given = pair_sum(at, lows + highs)
    return (*final_sum(kept, lax.ppermute(given, "seq", to(0, 0, 1))), beside)


def unpack_kernel(x_ref, o_ref):
    half = x_ref.shape[2]
    pick = onehot(
        1024,
        512,
        lambda r, c: ((r & 3) == (c >> 7)) & ((r >> 4) == ((c >> 1) & 63)) & (((r >> 2) & 1) == (c & 1)),
    )
    rows = x_ref[...].astype(F32)
    for n in range(2):
        part = rows[:, n * 8 : (n + 1) * 8].reshape(1024, half).astype(BF)
        part = mm(part.T, pick).astype(BF)
        for f in range(4):
            o_ref[:, f * 256 + n * 128 : f * 256 + (n + 1) * 128] = part[:, f * 128 : (f + 1) * 128]


def unpack(x):
    half = x.shape[2]
    return pl.pallas_call(
        unpack_kernel,
        out_shape=jax.ShapeDtypeStruct((half, 1024), BF),
        compiler_params=params(32),
        cost_estimate=hint(10**6, 10**6),
        name="unpack_rows",
    )(x)


def shards(hidden, out_cotangent, qkv_weight, out_weight):
    tokens, width = hidden.shape
    local = qkv_weight.shape[2]
    n_seq = lax.axis_size("seq")
    w_rows = qkv_weight.transpose(1, 2, 0).reshape(3 * local, width)
    place = lax.axis_index("seq").astype(jnp.int32)
    core = (place % 2).reshape(1)
    at = jnp.stack([place // 8 % 4, place // 2 % 4, place // 32])

    def to_patches(rows):
        return lax.all_to_all(rows.reshape(n_seq, 16, width), "seq", split_axis=0, concat_axis=0, tiled=True).reshape(tokens, width)

    def to_frames(rows):
        rows = rows.reshape(2 * n_seq, 16, width // 2)
        return lax.all_to_all(rows, ("seq", "tp"), split_axis=0, concat_axis=0, tiled=True)

    w_halves = turn_weights(w_rows)
    arrived = to_patches(pack(hidden, out_cotangent, 0))
    send = pack(hidden, out_cotangent, 1)
    arrived, send, w_halves = lax.optimization_barrier((arrived, send, w_halves))
    second = to_patches(send)
    terms = attend(arrived, w_rows, out_weight)
    other = weight_grads(1 - core, terms)
    mine = weight_grads(core, terms)
    dqkv = terms[3]
    second, other, mine, dqkv = lax.optimization_barrier((second, other, mine, dqkv))
    terms = attend(second, w_rows, out_weight)
    sending = input_grads(dqkv, terms[3], w_halves)
    terms, sending = lax.optimization_barrier((terms, sending))
    returned = to_frames(sending)
    other = weight_grads(1 - core, terms, other)
    from_peer = lax.ppermute(other, "seq", [(i, i ^ 1) for i in range(n_seq)])
    mine = weight_grads(core, terms, mine, 10**11)
    shape = (32 * 24, 2 * width)
    qkv_grad, out_grad, returned = sum_over_chips(mine.reshape(shape), from_peer.reshape(shape), at, returned)
    return (unpack(returned).T, qkv_grad.transpose(1, 0, 2), out_grad)


def solution(mesh):
    return jax.shard_map(
        shards,
        mesh=mesh,
        in_specs=(P("seq", None), P("seq", None), P(None, None, "tp"), P("tp", None)),
        out_specs=(P("seq", "tp"), P("seq", None, "tp"), P(("tp", "seq"), None)),
        check_vma=False,
    )
```

```python
import functools

import jax
import jax.numpy as jnp
from jax import lax
from jax.experimental import pallas as pl
from jax.experimental.pallas import tpu as pltpu
from jax.sharding import PartitionSpec as P

HEAD_DIM = 88
P_SIZE = 256
MIB = 1024 * 1024
BF = jnp.bfloat16
F32 = jnp.float32
NN = (((1,), (0,)), ((), ()))
NT = (((1,), (1,)), ((), ()))
TN = (((0,), (0,)), ((), ()))


def mm(a, b, dims=NN):
    return lax.dot_general(a, b, dims, preferred_element_type=F32)


def onehot(rows, cols, match):
    r = lax.broadcasted_iota(jnp.int32, (rows, cols), 0)
    c = lax.broadcasted_iota(jnp.int32, (rows, cols), 1)
    return jnp.where(match(r, c), 1.0, 0.0).astype(BF)


def hint(flops, size):
    return pl.CostEstimate(flops=flops, bytes_accessed=size, transcendentals=0)


def params(mib):
    return pltpu.CompilerParams(vmem_limit_bytes=mib * MIB)


def pack_kernel(x_ref, c_ref, o_ref, perm_ref):
    width = x_ref.shape[2]

    @pl.when(pl.program_id(0) == 0)
    def _():
        perm_ref[...] = onehot(
            512,
            512,
            lambda r, c: ((r >> 4) == ((c >> 1) & 31))
            & (((r >> 3) & 1) == (c >> 8))
            & (((r >> 2) & 1) == (c & 1))
            & ((r & 3) == ((c >> 6) & 3)),
        )

    rows = jnp.concatenate([x_ref[...].reshape(256, width), c_ref[...].reshape(256, width)], axis=0)
    o_ref[...] = mm(perm_ref[...], rows).astype(BF)


def pack(x, c, part):
    tokens, width = x.shape
    spec = pl.BlockSpec((4, 64, width), lambda b: (0, 2 * part + b, 0))
    return pl.pallas_call(
        pack_kernel,
        grid=(2,),
        in_specs=[spec, spec],
        out_specs=pl.BlockSpec((512, width), lambda b: (b, 0)),
        out_shape=jax.ShapeDtypeStruct((tokens, width), BF),
        scratch_shapes=[pltpu.VMEM((512, 512), BF)],
        compiler_params=params(60),
        cost_estimate=hint(10**6, 10**6),
        name="pack_rows",
    )(x.reshape(4, P_SIZE, width), c.reshape(4, P_SIZE, width))


def turn_kernel(w_ref, halves_ref):
    half = halves_ref.shape[2]
    halves_ref[0] = w_ref[:, :half]
    halves_ref[1] = w_ref[:, half:]


def turn_weights(w):
    cols, width = w.shape
    return pl.pallas_call(
        turn_kernel,
        grid=(3,),
        in_specs=[pl.BlockSpec((cols // 3, width), lambda j: (j, 0))],
        out_specs=pl.BlockSpec((2, cols // 3, width // 2), lambda j: (0, j, 0)),
        out_shape=jax.ShapeDtypeStruct((2, cols, width // 2), BF),
        compiler_params=params(60),
        cost_estimate=hint(10**6, 10**6),
        name="turn_weights",
    )(w)


def spread(from_ref, to_ref, rows, offset):
    for core in range(2):
        for place in range(32):
            device = 2 * place + core
            to_ref[core, place * 24 + offset : place * 24 + offset + rows, :] = from_ref[device * rows : (device + 1) * rows, :]


def attend_kernel(
    x_any,
    w_any,
    wo_any,
    xt_ref,
    low_ref,
    high_ref,
    dqkv_ref,
    cot_ref,
    sorted_ref,
    qkv_ref,
    grad_ref,
    turned_ref,
    wide_ref,
    attn_ref,
    upper_ref,
    lower_ref,
    patch_ref,
    x_ref,
    w_ref,
    wo_ref,
    sems,
):
    heads = grad_ref.shape[0]
    local = heads * HEAD_DIM
    scale = HEAD_DIM ** -0.5
    p = pl.program_id(0)
    copies = [
        pltpu.make_async_copy(source, target, sems.at[n])
        for n, (source, target) in enumerate(((x_any, x_ref), (w_any, w_ref), (wo_any, wo_ref)))
    ]

    @pl.when(p == 0)
    def _():
        for copy in copies:
            copy.start()
        copies[0].wait()
        perm = onehot(
            256,
            256,
            lambda r, c: ((r >> 6) == ((c >> 2) & 3)) & (((r >> 2) & 15) == (c >> 4)) & ((r & 3) == (c & 3)),
        )
        for b in range(4):
            part = mm(perm, x_ref[b * 256 : (b + 1) * 256, :]).astype(BF)
            for q in range(4):
                sorted_ref[q, b * 64 : (b + 1) * 64, :] = part[q * 64 : (q + 1) * 64, :]
        wide_ref[...] = jnp.zeros_like(wide_ref)
        upper_ref[...] = jnp.zeros_like(upper_ref)
        lower_ref[...] = jnp.zeros_like(lower_ref)
        copies[1].wait()
        copies[2].wait()

    xt = sorted_ref[p].T
    for j in range(3):
        part = mm(w_ref[j * local : (j + 1) * local, :], xt)
        qkv_ref[j * heads : (j + 1) * heads] = part.reshape(heads, HEAD_DIM, 256).astype(BF)
    cot = sorted_ref[2 + p]
    cot_ref[0] = cot
    grad_ref[...] = mm(wo_ref[...], cot.T).reshape(heads, HEAD_DIM, 256).astype(BF)
    turned_ref[...] = xt.astype(F32)
    spread(turned_ref, wide_ref, 22, 0)
    xt_ref[...] = wide_ref[...].astype(BF)
    for h in range(heads):
        query = qkv_ref[h]
        key = qkv_ref[heads + h]
        value = qkv_ref[2 * heads + h]
        gout = grad_ref[h]
        scores = mm(key.T, query) * scale
        expo = jnp.exp(scores - jnp.max(scores, axis=0, keepdims=True))
        prob = expo * (1.0 / jnp.sum(expo, axis=0, keepdims=True))
        weights = prob.astype(BF)
        attn_ref[h * HEAD_DIM : (h + 1) * HEAD_DIM, :] = mm(value, weights)
        dvalue = mm(gout, weights, NT)
        dweights = mm(value.T, gout)
        mean = jnp.sum(prob * dweights, axis=0, keepdims=True)
        dscores = (prob * (dweights - mean) * scale).astype(BF)
        dquery = mm(key, dscores)
        dkey = mm(query, dscores, NT)
        for j, term in enumerate((dquery, dkey, dvalue)):
            at = j * local + h * HEAD_DIM
            patch_ref[at : at + HEAD_DIM, :] = term
    dqkv_ref[0, :, : 3 * local] = patch_ref[...].astype(BF).T
    dqkv_ref[0, :, 3 * local :] = jnp.zeros((256, dqkv_ref.shape[2] - 3 * local), BF)
    spread(attn_ref, upper_ref, 11, 0)
    spread(attn_ref, lower_ref, 11, 11)
    low_ref[...] = upper_ref[...].astype(BF)
    high_ref[...] = lower_ref[...].astype(BF)


def attend(x, w, wo):
    tokens, width = x.shape
    local = wo.shape[0]
    heads = local // HEAD_DIM
    cols = -(-3 * local // 128) * 128
    spread_spec = pl.BlockSpec((2, 768, 256), lambda p: (0, 0, p))
    spread_shape = jax.ShapeDtypeStruct((2, 768, 512), BF)
    return pl.pallas_call(
        attend_kernel,
        grid=(2,),
        in_specs=[pl.BlockSpec(memory_space=pl.ANY)] * 3,
        out_specs=[
            spread_spec,
            spread_spec,
            spread_spec,
            pl.BlockSpec((1, 256, cols), lambda p: (p, 0, 0)),
            pl.BlockSpec((1, 256, width), lambda p: (p, 0, 0)),
        ],
        out_shape=[
            spread_shape,
            spread_shape,
            spread_shape,
            jax.ShapeDtypeStruct((2, 256, cols), BF),
            jax.ShapeDtypeStruct((2, 256, width), BF),
        ],
        scratch_shapes=[
            pltpu.VMEM((4, 256, width), BF),
            pltpu.VMEM((3 * heads, HEAD_DIM, 256), BF),
            pltpu.VMEM((heads, HEAD_DIM, 256), BF),
            pltpu.VMEM((width, 256), F32),
            pltpu.VMEM((2, 768, 256), F32),
            pltpu.VMEM((local, 256), F32),
            pltpu.VMEM((2, 768, 256), F32),
            pltpu.VMEM((2, 768, 256), F32),
            pltpu.VMEM((3 * local, 256), F32),
            pltpu.VMEM(x.shape, BF),
            pltpu.VMEM(w.shape, BF),
            pltpu.VMEM(wo.shape, BF),
            pltpu.SemaphoreType.DMA((3,)),
        ],
        compiler_params=params(60),
        cost_estimate=hint(10**6, 10**6),
        name="attend",
    )(x, w, wo)


def input_kernel(first_any, second_any, w_any, send_any, dqkv_ref, w_ref, rows_ref, part_ref, sems):
    cols, half = w_ref.shape[1:]
    copies = [
        pltpu.make_async_copy(source, target, sems.at[n])
        for n, (source, target) in enumerate(
            (
                (first_any, dqkv_ref.at[0:2]),
                (second_any, dqkv_ref.at[2:4]),
                (w_any.at[0], w_ref.at[0]),
                (w_any.at[1], w_ref.at[1]),
            )
        )
    ]
    for copy in copies:
        copy.start()
    perm = onehot(
        256,
        256,
        lambda r, c: ((c >> 6) == ((r >> 2) & 3)) & (((c >> 2) & 15) == (r >> 4)) & ((r & 3) == (c & 3)),
    )
    copies[0].wait()
    copies[1].wait()
    for b in range(4):
        rows = dqkv_ref[:, b * 64 : (b + 1) * 64, :cols].reshape(256, cols)
        rows_ref[b * 256 : (b + 1) * 256, :] = mm(perm, rows).astype(BF)
    outs = [pltpu.make_async_copy(part_ref.at[t], send_any.at[:, t], sems.at[4 + t]) for t in range(2)]
    for t in range(2):
        copies[2 + t].wait()
        for b in range(2):
            part = mm(rows_ref[b * 512 : (b + 1) * 512, :], w_ref[t])
            part_ref[t, b * 32 : (b + 1) * 32] = part.astype(BF).reshape(32, 16, half)
        outs[t].start()
    for out in outs:
        out.wait()


def input_grads(first, second, w):
    cols, half = w.shape[1:]
    hbm = pl.BlockSpec(memory_space=pl.ANY)
    return pl.pallas_call(
        input_kernel,
        in_specs=[hbm, hbm, hbm],
        out_specs=hbm,
        out_shape=jax.ShapeDtypeStruct((64, 2, 16, half), BF),
        scratch_shapes=[
            pltpu.VMEM((4, *first.shape[1:]), BF),
            pltpu.VMEM(w.shape, BF),
            pltpu.VMEM((1024, cols), BF),
            pltpu.VMEM((2, 64, 16, half), BF),
            pltpu.SemaphoreType.DMA((6,)),
        ],
        compiler_params=params(60),
        cost_estimate=hint(10**6, 10**6),
        name="input_grads",
    )(first, second, w)


def weights_kernel(core_ref, xt_ref, low_ref, high_ref, dqkv_ref, c_ref, *refs):
    o_ref = refs[-1]
    places = o_ref.shape[0]
    half = c_ref.shape[1] // 2
    cols = 3 * half

    def put(value, at):
        value = value.reshape(places, 24, value.shape[1])
        if len(refs) == 2:
            value += refs[0][:, :, at].astype(F32)
        o_ref[:, :, at] = value.astype(BF)

    put(mm(xt_ref[0], dqkv_ref[:, :cols]), slice(0, cols))
    put(mm(low_ref[0], c_ref[:, :half]) + mm(high_ref[0], c_ref[:, half:]), slice(cols, cols + half))


def weight_grads(core, terms, before=None, flops=10**6):
    xt, low, high, dqkv, cot = terms
    tokens = xt.shape[2]
    dqkv, cot = dqkv.reshape(tokens, -1), cot.reshape(tokens, -1)
    width = cot.shape[1]
    once = pl.Buffered(buffer_count=1)
    rows_spec = pl.BlockSpec((1, 384, tokens), lambda s, core: (core[0], s, 0))
    out_spec = pl.BlockSpec((16, 24, 2 * width), lambda s, core: (s, 0, 0))
    given = [] if before is None else [before]
    return pl.pallas_call(
        weights_kernel,
        grid_spec=pltpu.PrefetchScalarGridSpec(
            num_scalar_prefetch=1,
            grid=(2,),
            in_specs=[
                rows_spec,
                rows_spec,
                rows_spec,
                pl.BlockSpec(dqkv.shape, lambda s, core: (0, 0), pipeline_mode=once),
                pl.BlockSpec(cot.shape, lambda s, core: (0, 0), pipeline_mode=once),
            ]
            + [out_spec] * len(given),
            out_specs=out_spec,
        ),
        out_shape=jax.ShapeDtypeStruct((32, 24, 2 * width), BF),
        compiler_params=params(60),
        cost_estimate=hint(flops, 10**6),
        name="weight_grads",
    )(core, xt, low, high, dqkv, cot, *given)


def core_kernel(at_ref, mine_low, other_low, mine_high, other_high, *outs):
    k = pl.program_id(0)
    for group, terms in enumerate(((mine_low, other_low), (mine_high, other_high))):
        total = (terms[0][...].astype(F32) + terms[1][...].astype(F32)).astype(BF).reshape(outs[0].shape)
        own, after, before, left, right = outs[5 * group : 5 * group + 5]

        @pl.when(k == 0)
        def _():
            own[...] = total

        @pl.when(k == 1)
        def _():
            after[...] = total

        @pl.when(k == 3)
        def _():
            before[...] = total

        @pl.when(k == 2)
        def _():
            left[...] = total[0]
            right[...] = total[1]


def core_sum(at, mine, arrived):
    width = mine.shape[4] // 2
    shape = (2, 4, 24, width)
    low = pl.BlockSpec((2, 1, 4, 24, width), lambda k, at: (0, (at[0] + k) % 4, 0, 0, 0))
    high = pl.BlockSpec((2, 4, 1, 24, width), lambda k, at: (0, 0, (at[1] + k) % 4, 0, 1))
    shapes = ([shape] * 3 + [shape[1:]] * 2) * 2
    return pl.pallas_call(
        core_kernel,
        grid_spec=pltpu.PrefetchScalarGridSpec(
            num_scalar_prefetch=1,
            grid=(4,),
            in_specs=[low, low, high, high],
            out_specs=[pl.BlockSpec(shape, lambda k, at, n=len(shape): (0,) * n) for shape in shapes],
        ),
        out_shape=[jax.ShapeDtypeStruct(shape, BF) for shape in shapes],
        compiler_params=params(40),
        cost_estimate=hint(10**6, 10**6),
        name="core_sum",
    )(at, mine, arrived, mine, arrived)


def pass_kernel(*refs):
    ins, outs = refs[:8], refs[8:]
    for group in range(2):
        after, before, left, right = ins[4 * group : 4 * group + 4]
        outs[2 * group][0] = (after[0].astype(F32) + left[...].astype(F32)).astype(BF)
        outs[2 * group][1] = after[1]
        outs[2 * group + 1][0] = before[0]
        outs[2 * group + 1][1] = (before[1].astype(F32) + right[...].astype(F32)).astype(BF)


def pass_on(*terms):
    return pl.pallas_call(
        pass_kernel,
        out_shape=[jax.ShapeDtypeStruct(terms[0].shape, BF)] * 4,
        compiler_params=params(24),
        cost_estimate=hint(10**6, 10**6),
        name="pass_on",
    )(*terms)


def ring_kernel(at_ref, *refs):
    k = pl.program_id(0)
    outs = refs[6:]
    for group in range(2):
        total = refs[3 * group][...].astype(F32)
        for term in refs[3 * group + 1 : 3 * group + 3]:
            total += term[...].astype(F32)
        for q in range(4):

            @pl.when(k == q)
            def _():
                outs[4 * group + q][...] = total.astype(BF).reshape(outs[q].shape)


def ring_sum(at, lows, highs):
    width = lows[0].shape[3]
    shape = (2, 24, width)
    low = pl.BlockSpec((2, 1, 24, width), lambda k, at: (0, (at[1] + k) % 4, 0, 0))
    high = pl.BlockSpec((2, 1, 24, width), lambda k, at: (0, (at[0] + k) % 4, 0, 0))
    return pl.pallas_call(
        ring_kernel,
        grid_spec=pltpu.PrefetchScalarGridSpec(
            num_scalar_prefetch=1,
            grid=(4,),
            in_specs=[low] * 3 + [high] * 3,
            out_specs=[pl.BlockSpec(shape, lambda k, at: (0, 0, 0))] * 8,
        ),
        out_shape=[jax.ShapeDtypeStruct(shape, BF)] * 8,
        compiler_params=params(40),
        cost_estimate=hint(10**6, 10**6),
        name="ring_sum",
    )(at, *lows, *highs)


def pair_kernel(at_ref, *refs):
    mine_ref, other_ref = refs[8:]
    for group in range(2):
        total = refs[4 * group][...].astype(F32)
        for term in refs[4 * group + 1 : 4 * group + 4]:
            total += term[...].astype(F32)
        z = at_ref[2]
        mine_ref[group] = jnp.where(z == 0, total[0], total[1])
        other_ref[group] = jnp.where(z == 0, total[1], total[0]).astype(BF)


def pair_sum(at, terms):
    shape = terms[0].shape
    return pl.pallas_call(
        pair_kernel,
        in_specs=[pl.BlockSpec(memory_space=pltpu.SMEM)] + [pl.BlockSpec(memory_space=pltpu.VMEM)] * 8,
        out_shape=[jax.ShapeDtypeStruct(shape, F32), jax.ShapeDtypeStruct(shape, BF)],
        compiler_params=params(16),
        name="pair_sum",
    )(at, *terms)


def final_kernel(mine_ref, other_ref, qkv_ref, out_ref):
    half = out_ref.shape[1] // 2
    low = mine_ref[0] + other_ref[0].astype(F32)
    high = mine_ref[1] + other_ref[1].astype(F32)
    qkv_ref[0] = low[:22, :half]
    qkv_ref[1] = low[:22, half:]
    qkv_ref[2] = high[:22, :half]
    out_ref[:, :half] = high[:11, half:]
    out_ref[:, half:] = high[11:22, half:]


def final_sum(mine, other):
    width = mine.shape[2]
    return pl.pallas_call(
        final_kernel,
        out_shape=[jax.ShapeDtypeStruct((3, 22, width // 2), F32), jax.ShapeDtypeStruct((11, width), F32)],
        compiler_params=params(16),
        name="final_sum",
    )(mine, other)


def sum_over_chips(mine, arrived, at, beside):
    width = mine.shape[1] // 2
    mine, arrived = (a.reshape(2, 4, 4, 24, 2 * width) for a in (mine, arrived))

    def to(step_x, step_y, flip=0):
        pairs = []
        for i in range(64):
            z, x, y, core = i // 32, i // 8 % 4, i // 2 % 4, i % 2
            pairs.append((i, (((z ^ flip) * 4 + (x + step_x) % 4) * 4 + (y + step_y) % 4) * 2 + core))
        return pairs

    first = core_sum(at, mine, arrived)
    steps = ((1, 0), (-1, 0), (0, 1), (0, -1))
    halves = [lax.ppermute(first[n], "seq", to(*step)) for n, step in zip((3, 4, 8, 9), steps)]
    passed = pass_on(first[1], first[2], *halves[:2], first[6], first[7], *halves[2:])
    passed = [lax.ppermute(value, "seq", to(*step)) for value, step in zip(passed, steps)]
    second = ring_sum(at, [first[0], *passed[:2]], [first[5], *passed[2:]])
    lows = [second[0]] + [lax.ppermute(second[k], "seq", to(0, k)) for k in (1, 2, 3)]
    highs = [second[4]] + [lax.ppermute(second[4 + k], "seq", to(k, 0)) for k in (1, 2, 3)]
    kept, given = pair_sum(at, lows + highs)
    return (*final_sum(kept, lax.ppermute(given, "seq", to(0, 0, 1))), beside)


def unpack_kernel(x_ref, o_ref):
    half = x_ref.shape[2]
    pick = onehot(
        1024,
        512,
        lambda r, c: ((r & 3) == (c >> 7)) & ((r >> 4) == ((c >> 1) & 63)) & (((r >> 2) & 1) == (c & 1)),
    )
    rows = x_ref[...].astype(F32)
    for n in range(2):
        part = rows[:, n * 8 : (n + 1) * 8].reshape(1024, half).astype(BF)
        part = mm(part.T, pick).astype(BF)
        for f in range(4):
            o_ref[:, f * 256 + n * 128 : f * 256 + (n + 1) * 128] = part[:, f * 128 : (f + 1) * 128]


def unpack(x):
    half = x.shape[2]
    return pl.pallas_call(
        unpack_kernel,
        out_shape=jax.ShapeDtypeStruct((half, 1024), BF),
        compiler_params=params(32),
        cost_estimate=hint(10**6, 10**6),
        name="unpack_rows",
    )(x)


def shards(hidden, out_cotangent, qkv_weight, out_weight):
    tokens, width = hidden.shape
    local = qkv_weight.shape[2]
    n_seq = lax.axis_size("seq")
    w_rows = qkv_weight.transpose(1, 2, 0).reshape(3 * local, width)
    place = lax.axis_index("seq").astype(jnp.int32)
    core = (place % 2).reshape(1)
    at = jnp.stack([place // 8 % 4, place // 2 % 4, place // 32])

    def to_patches(rows):
        return lax.all_to_all(rows.reshape(n_seq, 16, width), "seq", split_axis=0, concat_axis=0, tiled=True).reshape(tokens, width)

    def to_frames(rows):
        rows = rows.reshape(2 * n_seq, 16, width // 2)
        return lax.all_to_all(rows, ("seq", "tp"), split_axis=0, concat_axis=0, tiled=True)

    w_halves = turn_weights(w_rows)
    arrived = to_patches(pack(hidden, out_cotangent, 0))
    send = pack(hidden, out_cotangent, 1)
    arrived, send, w_halves = lax.optimization_barrier((arrived, send, w_halves))
    second = to_patches(send)
    terms = attend(arrived, w_rows, out_weight)
    other = weight_grads(1 - core, terms)
    mine = weight_grads(core, terms)
    dqkv = terms[3]
    second, other, mine, dqkv = lax.optimization_barrier((second, other, mine, dqkv))
    terms = attend(second, w_rows, out_weight)
    sending = input_grads(dqkv, terms[3], w_halves)
    terms, sending = lax.optimization_barrier((terms, sending))
    returned = to_frames(sending)
    other = weight_grads(1 - core, terms, other)
    from_peer = lax.ppermute(other, "seq", [(i, i ^ 1) for i in range(n_seq)])
    mine = weight_grads(core, terms, mine, 10**11)
    shape = (32 * 24, 2 * width)
    qkv_grad, out_grad, returned = sum_over_chips(mine.reshape(shape), from_peer.reshape(shape), at, returned)
    return (unpack(returned).T, qkv_grad.transpose(1, 0, 2), out_grad)


def solution(mesh):
    return jax.shard_map(
        shards,
        mesh=mesh,
        in_specs=(P("seq", None), P("seq", None), P(None, None, "tp"), P("tp", None)),
        out_specs=(P("seq", "tp"), P("seq", None, "tp"), P(("tp", "seq"), None)),
        check_vma=False,
    )
```
